32 devices in a mesh: fsdp: 8 (over z, y), rep: 4 (over x, core).
Axes of the slice: x: 2, y: 2, z: 4, core: 2. Of those that a mesh axis runs over, the one named last changes fastest.
Arguments:
- tokens: bfloat16 [8192, 1088], P(('fsdp', 'rep')), may hold values from -6 to 6
- lengths: int32 [32, 4], P(('fsdp', 'rep')), may hold values from 0 to 256, as said below
- attn_weights: bfloat16 [4352, 1088], P(('fsdp', 'rep'))
- vectors: bfloat16 [13056], P(('fsdp', 'rep'))
- up_weights: bfloat16 [4352, 1088], P(('fsdp', 'rep')), may hold values from -0.1875 to 0.1875
- down_weights: bfloat16 [4352, 1088], P(('fsdp', 'rep')), may hold values from -0.09375 to 0.09375
- cotangent: bfloat16 [8192, 1088], P(('fsdp', 'rep')), may hold values from -6 to 6
Outputs:
- out: bfloat16 [8192, 1088], P(('fsdp', 'rep'))
- grad_tokens: bfloat16 [8192, 1088], P(('fsdp', 'rep'))
- grad_attn_weights: float32 [4352, 1088], P(('fsdp', 'rep'))
- grad_vectors: float32 [13056], P(('fsdp', 'rep'))
- grad_up_weights: float32 [4352, 1088], P(('fsdp', 'rep'))
- grad_down_weights: float32 [4352, 1088], P(('fsdp', 'rep'))
The draws below stay inside these ranges and needn't reach their ends.
Inputs may be any that keep to these rules, and one draw needn't show every extreme that they name: `lengths`: row p gives, in order from slot 0, the sequences packed into the blocks of pack p, which is held by device p of fsdp+rep (fsdp major); a row sums to at most 256 and the slots after its sum are empty; in every draw one row, drawn from the seed, is a single sequence of 256 tokens followed by zeros.
All inputs are finite; a program needn't handle non-finite values.
Results may differ from the reference program's by a relative error of at most 0.013.
Values may be sent and summed in bfloat16 or wider, within the bound.
A program may use at most 192 MiB of HBM per device.

```python
import jax
import jax.numpy as jnp
from jax import lax

D = 1088
HEADS = 17
HEAD_DIM = 64
FF = 4352
SEQS_DEV = 4
SLOTS = 256
PACKS = 32
TOKENS = 8192


def draw_lengths(key, part):
    key_totals, key_cuts, key_full = jax.random.split(key, 3)
    totals = jax.random.randint(key_totals, (PACKS,), 1, SLOTS)
    cut_points = jnp.sort(jax.random.randint(key_cuts, (PACKS, SEQS_DEV - 1), 0, totals[:, None] + 1), axis=1)
    bounds = jnp.concatenate([jnp.zeros((PACKS, 1), jnp.int32), cut_points.astype(jnp.int32), totals[:, None].astype(jnp.int32)], axis=1)
    pieces = bounds[:, 1:] - bounds[:, :-1]
    full_pack = jax.random.randint(key_full, (), 0, PACKS)
    single = jnp.where(jnp.arange(SEQS_DEV) == 0, SLOTS, 0).astype(jnp.int32)
    chosen = (jnp.arange(PACKS) == full_pack)[:, None]
    return jnp.where(chosen, single[None, :], pieces).astype(jnp.int32)


def draw_attn_weights(key, part):
    row_ids = jnp.arange(4 * D)[:, None]
    row_scale = jnp.where(row_ids < 3 * D, 1.5, 3.0) * D ** (-0.5)
    base_draw = jax.random.normal(key, (4 * D, D), jnp.float32)
    return (base_draw * row_scale).astype(jnp.bfloat16)


def draw_vectors(key, part):
    flat_index = jnp.arange(8 * D + FF)
    segment = flat_index // D
    is_gain = (segment == 0) | (segment == 5)
    key_gain, key_bias = jax.random.split(key)
    spread = jax.random.uniform(key_gain, (8 * D + FF,), jnp.float32, -0.5, 0.5)
    bias_draw = 0.3 * jax.random.normal(key_bias, (8 * D + FF,), jnp.float32)
    return jnp.where(is_gain, 1.0 + spread, bias_draw).astype(jnp.bfloat16)


def steps_of(rng, dims, shards, low, top_value):
    def one(position, parts):
        heights = jax.random.uniform(jax.random.fold_in(jax.random.fold_in(rng, 6), position), (parts,), jnp.float32, low / len(shards), top_value / len(shards))
        return jnp.repeat(jnp.exp(heights), dims[position] // parts).reshape((-1,) + (1,) * (len(dims) - position - 1))

    loudness = one(*shards[0])
    for cut in shards[1:]:
        loudness = loudness * one(*cut)
    return loudness


def normal_values(stream_key, extent, scale, bound, shards=(), kind=jnp.bfloat16):
    loudness = steps_of(stream_key, extent, shards, -0.22, 0.18) if shards else 1.0
    values = jax.random.normal(stream_key, extent, jnp.float32) * scale * loudness
    return jnp.minimum(jnp.maximum(values, -bound), bound).astype(kind)


def setup_inputs(seed: int = 0) -> dict:
    key_list = jax.random.split(jax.random.key(seed), 8)
    return {
        "tokens": normal_values(key_list[0], (TOKENS, D), 1.0, 6.0, ((0, 32),)),
        "lengths": draw_lengths(jax.random.fold_in(key_list[7], 71), 0),
        "attn_weights": draw_attn_weights(jax.random.fold_in(key_list[7], 71), 0),
        "vectors": draw_vectors(jax.random.fold_in(key_list[7], 71), 0),
        "up_weights": normal_values(key_list[4], (FF, D), D ** -0.5, 0.1875, ((0, 32),)),
        "down_weights": normal_values(key_list[5], (FF, D), FF ** -0.5, 0.09375, ((0, 32),)),
        "cotangent": normal_values(key_list[6], (TOKENS, D), 1.0, 6.0, ((0, 32),)),
    }


@jax.custom_vjp
def low(v):
    return lax.optimization_barrier(v.astype(jnp.bfloat16)).astype(jnp.float32)

@jax.custom_vjp
def low_back(v):
    return v

def low_keep(v):
    return (low(v), None)

def low_pass(kept, grad):
    return (grad,)

def back_keep(v):
    return (v, None)

def back_low(kept, grad):
    return (low(grad),)
low.defvjp(low_keep, low_pass)
low_back.defvjp(back_keep, back_low)
epsilon = 1e-05
negative = -1e+30
highest = lax.Precision.HIGHEST

def layer_norm(values, gain, shift):
    center = values - lax.optimization_barrier(jnp.mean(values, axis=-1, keepdims=True))
    variance = lax.optimization_barrier(jnp.mean(center * center, axis=-1, keepdims=True))
    return center * lax.rsqrt(variance + epsilon) * gain + shift

def product(left, right):
    return jnp.dot(left, right, precision=highest)

def pack_forward(inputs, lengths, attn_weights, vectors, up_weights, down_weights):
    slot_count = inputs.shape[0]
    gain_one = vectors[0:D]
    shift_one = vectors[D:2 * D]
    query_bias = vectors[2 * D:3 * D]
    value_bias = vectors[3 * D:4 * D]
    out_bias = vectors[4 * D:5 * D]
    gain_two = vectors[5 * D:6 * D]
    shift_two = vectors[6 * D:7 * D]
    up_bias = vectors[7 * D:7 * D + FF]
    down_bias = vectors[7 * D + FF:]
    hidden_one = low(layer_norm(inputs, gain_one, shift_one))
    qkv_bias = jnp.concatenate([query_bias, jnp.zeros((D,), jnp.float32), value_bias])
    projected = low(low_back(product(hidden_one, attn_weights[:3 * D].T) + qkv_bias))
    queries = projected[:, :D].reshape(slot_count, HEADS, HEAD_DIM)
    key_heads = projected[:, D:2 * D].reshape(slot_count, HEADS, HEAD_DIM)
    value_heads = projected[:, 2 * D:].reshape(slot_count, HEADS, HEAD_DIM)
    positions = jnp.arange(slot_count, dtype=jnp.int32)
    seq_ends = jnp.cumsum(lengths).astype(jnp.int32)
    segment = lax.optimization_barrier(jnp.sum((positions[:, None] >= seq_ends[None, :]).astype(jnp.int32), axis=1))
    allowed = (segment[:, None] == segment[None, :]) & (positions[None, :] <= positions[:, None])
    raw_scores = low_back(jnp.einsum('qhd,khd->hqk', queries, key_heads, precision=highest))
    scores = jnp.where(allowed[None], raw_scores * HEAD_DIM ** (-0.5), negative)
    prob_low = low(jax.nn.softmax(scores, axis=-1))
    mixed = jnp.einsum('hqk,khd->qhd', prob_low, value_heads, precision=highest).reshape(slot_count, D)
    mixed = low(low_back(mixed))
    attended = low_back(product(mixed, attn_weights[3 * D:].T) + out_bias)
    residual = inputs + attended
    hidden_two = low(layer_norm(residual, gain_two, shift_two))
    upward = low_back(product(hidden_two, up_weights.T) + up_bias)
    activated = low(jax.nn.gelu(upward, approximate=False))
    downward = low_back(product(activated, down_weights) + down_bias)
    live_rows = (positions < seq_ends[-1]).astype(jnp.float32)[:, None]
    return (residual + downward) * live_rows

def reference(tokens, lengths, attn_weights, vectors, up_weights, down_weights, cotangent):
    inputs = tokens.astype(jnp.float32).reshape(PACKS, SLOTS, D)
    params = (attn_weights.astype(jnp.float32), vectors.astype(jnp.float32), up_weights.astype(jnp.float32), down_weights.astype(jnp.float32))

    def forward(pack_inputs, weight_set):

        def one_pack(pack_pair):
            return pack_forward(pack_pair[0], pack_pair[1], weight_set[0], weight_set[1], weight_set[2], weight_set[3])
        return lax.map(jax.checkpoint(one_pack), (pack_inputs, lengths))
    results, pullback = jax.vjp(forward, inputs, params)
    grad_inputs, weight_grads = pullback(cotangent.astype(jnp.float32).reshape(PACKS, SLOTS, D))
    return (results.reshape(TOKENS, D).astype(jnp.bfloat16), grad_inputs.reshape(TOKENS, D).astype(jnp.bfloat16), weight_grads[0], weight_grads[1], weight_grads[2], weight_grads[3])
```

```python
import jax
import jax.numpy as jnp
from jax import lax
from jax.sharding import PartitionSpec as P

HEADS = 17
HEAD_DIM = 64
FF = 4352


epsilon = 1e-05
negative = -1e30


def for_sending(shard):
    return jax.tree.map(lambda a: a.astype(jnp.bfloat16) if a.dtype == jnp.float32 else a, shard)


def contract(left, right, left_dim, right_dim):
    return lax.dot_general(
        left, right, (((left_dim,), (right_dim,)), ((), ())), preferred_element_type=jnp.float32
    )


def normalize(values):
    center = values - jnp.mean(values, axis=1, keepdims=True)
    scaled = lax.rsqrt(jnp.mean(center * center, axis=1, keepdims=True) + epsilon)
    return (center * scaled, scaled)


def norm_back(grad_normed, normed, scaled, gain):
    scaled_grad = grad_normed * gain
    return scaled * (
        scaled_grad
        - jnp.mean(scaled_grad, axis=1, keepdims=True)
        - normed * jnp.mean(scaled_grad * normed, axis=1, keepdims=True)
    )


def visible(segment, span_rows):
    row_ids = lax.iota(jnp.int32, span_rows)[:, None]
    col_ids = lax.iota(jnp.int32, segment.shape[0])[None, :]
    same_seg = segment[:, None] == segment[None, :]
    return same_seg & (col_ids <= row_ids)


def split_heads(matrix):
    return matrix.reshape(matrix.shape[0], HEADS, HEAD_DIM).transpose(1, 0, 2)


def join_heads(stacked):
    return stacked.transpose(1, 0, 2).reshape(stacked.shape[1], HEADS * HEAD_DIM)


def by_owner(matrix, outer_count, inner_count):
    slot_count, width = matrix.shape
    block_width = width // (outer_count * inner_count)
    return matrix.reshape(slot_count, outer_count, inner_count, block_width).transpose(0, 2, 1, 3)


def head_forward(head_parts, segment, span_rows):
    queries, key_heads, value_heads = head_parts
    factor = HEAD_DIM ** (-0.5)
    allowed = visible(segment, span_rows)
    raw_scores = contract(queries, key_heads, 1, 1)
    scores = jnp.where(allowed, raw_scores * factor, negative)
    row_peak = jnp.max(scores, axis=1, keepdims=True)
    exp_scores = jnp.exp(scores - row_peak)
    row_total = jnp.sum(exp_scores, axis=1, keepdims=True)
    prob_low = (exp_scores / row_total).astype(jnp.bfloat16)
    outputs = [contract(prob_low, value_heads, 1, 0)]
    totals = [row_peak + jnp.log(row_total)]
    return (jnp.concatenate(outputs, axis=0).astype(jnp.bfloat16), jnp.concatenate(totals, axis=0))


def head_backward(head_parts, segment, span_rows):
    queries, key_heads, value_heads, totals, grad_mixed = head_parts
    factor = HEAD_DIM ** (-0.5)
    grad_keys = jnp.zeros(key_heads.shape, jnp.float32)
    grad_values = jnp.zeros(value_heads.shape, jnp.float32)
    allowed = visible(segment, span_rows)
    grad_rows = grad_mixed[0:span_rows]
    raw_scores = contract(queries, key_heads, 1, 1)
    probs = jnp.where(allowed, jnp.exp(raw_scores * factor - totals[0:span_rows]), 0.0)
    grad_probs = contract(grad_rows, value_heads, 1, 1)
    row_delta = jnp.sum(probs * grad_probs, axis=1, keepdims=True)
    grad_scores = (probs * (grad_probs - row_delta) * factor).astype(jnp.bfloat16)
    grad_queries = [contract(grad_scores, key_heads, 1, 0)]
    grad_keys = grad_keys + contract(grad_scores, queries, 0, 0)
    grad_values = grad_values + contract(probs.astype(jnp.bfloat16), grad_rows, 0, 0)
    return (jnp.concatenate(grad_queries, axis=0), grad_keys, grad_values)


def local(tokens, lengths, attn_weights, vectors, up_weights, down_weights, cotangent):
    attn_full, vector_full = (
        lax.all_gather(attn_weights, ("fsdp", "rep"), axis=0, tiled=True),
        lax.all_gather(vectors, ("fsdp", "rep"), axis=0, tiled=True),
    )
    params = vector_full.astype(jnp.float32)
    slot_count, model_width = tokens.shape
    span_rows = min(512, slot_count)
    gain_one = params[0:model_width]
    shift_one = params[model_width : 2 * model_width]
    query_bias = params[2 * model_width : 3 * model_width]
    value_bias = params[3 * model_width : 4 * model_width]
    out_bias = params[4 * model_width : 5 * model_width]
    gain_two = params[5 * model_width : 6 * model_width]
    shift_two = params[6 * model_width : 7 * model_width]
    up_bias = params[7 * model_width : 7 * model_width + FF]
    down_bias = params[7 * model_width + FF :]
    seq_count = lengths.shape[1]
    upto = lax.iota(jnp.int32, seq_count)[:, None] >= lax.iota(jnp.int32, seq_count)[None, :]
    seq_ends = jnp.sum(jnp.where(upto, lengths, 0), axis=1)
    positions = lax.iota(jnp.int32, slot_count)
    segment = jnp.sum((positions[:, None] >= seq_ends[None, :]).astype(jnp.int32), axis=1)
    live_rows = (positions < seq_ends[-1]).astype(jnp.float32)[:, None]
    inputs = tokens.astype(jnp.float32)
    normed_one, scaled_one = normalize(inputs)
    hidden_one = (normed_one * gain_one + shift_one).astype(jnp.bfloat16)
    qkv_bias = jnp.concatenate([query_bias, jnp.zeros_like(query_bias), value_bias])
    projected = (contract(hidden_one, attn_full[: 3 * model_width], 1, 1) + qkv_bias).astype(
        jnp.bfloat16
    )
    queries = split_heads(projected[:, :model_width])
    key_heads = split_heads(projected[:, model_width : 2 * model_width])
    value_heads = split_heads(projected[:, 2 * model_width :])

    def attend_forward(head_parts):
        return head_forward(head_parts, segment, span_rows)

    mixed_heads, totals = lax.map(attend_forward, (queries, key_heads, value_heads))
    mixed = join_heads(mixed_heads)
    attended = contract(mixed, attn_full[3 * model_width :], 1, 1) + out_bias
    residual = inputs + attended
    normed_two, scaled_two = normalize(residual)
    hidden_two = (normed_two * gain_two + shift_two).astype(jnp.bfloat16)
    up_full, down_full = (
        lax.all_gather(up_weights, ("fsdp", "rep"), axis=0, tiled=True),
        lax.all_gather(down_weights, ("fsdp", "rep"), axis=0, tiled=True),
    )
    upward = contract(hidden_two, up_full, 1, 1) + up_bias
    activated = jax.nn.gelu(upward, approximate=False).astype(jnp.bfloat16)
    output = (residual + contract(activated, down_full, 1, 0) + down_bias) * live_rows
    up_back, down_back = (
        lax.all_gather(up_weights, ("fsdp", "rep"), axis=0, tiled=True),
        lax.all_gather(down_weights, ("fsdp", "rep"), axis=0, tiled=True),
    )
    grad_output = cotangent.astype(jnp.float32) * live_rows
    grad_down_in = grad_output.astype(jnp.bfloat16)
    grad_down_bias = jnp.sum(grad_down_in.astype(jnp.float32), axis=0)
    grad_act = contract(grad_down_in, down_back, 1, 1)

    def gelu_exact(values):
        return jax.nn.gelu(values, approximate=False)

    grad_upward = jax.vjp(gelu_exact, upward)[1](grad_act)[0]
    grad_up_in = grad_upward.astype(jnp.bfloat16)
    grad_up_bias = jnp.sum(grad_up_in.astype(jnp.float32), axis=0)
    grad_hidden_two = contract(grad_up_in, up_back, 1, 0)
    grad_gain_two = jnp.sum(grad_hidden_two * normed_two, axis=0)
    grad_shift_two = jnp.sum(grad_hidden_two, axis=0)
    grad_residual = grad_output + norm_back(grad_hidden_two, normed_two, scaled_two, gain_two)
    grad_attended = grad_residual.astype(jnp.bfloat16)
    attn_back = lax.all_gather(attn_weights, ("fsdp", "rep"), axis=0, tiled=True)
    grad_out_bias = jnp.sum(grad_attended.astype(jnp.float32), axis=0)
    grad_mixed = contract(grad_attended, attn_back[3 * model_width :], 1, 0).astype(jnp.bfloat16)

    def attend_backward(head_parts):
        return head_backward(head_parts, segment, span_rows)

    grad_q_heads, grad_k_heads, grad_v_heads = lax.map(
        attend_backward, (queries, key_heads, value_heads, totals, split_heads(grad_mixed))
    )
    grad_projected = jnp.concatenate(
        [join_heads(grad_q_heads), join_heads(grad_k_heads), join_heads(grad_v_heads)], axis=1
    ).astype(jnp.bfloat16)
    bias_sums = jnp.sum(grad_projected.astype(jnp.float32), axis=0)
    grad_hidden_one = contract(grad_projected, attn_back[: 3 * model_width], 1, 0)
    grad_gain_one = jnp.sum(grad_hidden_one * normed_one, axis=0)
    grad_shift_one = jnp.sum(grad_hidden_one, axis=0)
    grad_inputs = grad_residual + norm_back(grad_hidden_one, normed_one, scaled_one, gain_one)
    outer_count = lax.axis_size("fsdp")
    inner_count = lax.axis_size("rep")
    inner_index = lax.axis_index("rep")
    attn_left = jnp.concatenate([grad_projected, grad_attended], axis=1)
    attn_block = attn_left.shape[1] // (outer_count * inner_count)
    unit_block = grad_up_in.shape[1] // (outer_count * inner_count)
    bundle = jnp.concatenate(
        [
            by_owner(attn_left, outer_count, inner_count),
            by_owner(grad_up_in, outer_count, inner_count),
            by_owner(activated, outer_count, inner_count),
        ],
        axis=3,
    )
    bundle_width = bundle.shape[3]
    bundle = bundle.reshape(slot_count, inner_count * outer_count * bundle_width)
    received = lax.all_to_all(bundle, "rep", split_axis=1, concat_axis=0, tiled=True)
    received = received.reshape(received.shape[0], outer_count, bundle_width)
    attn_cols = received[:, :, :attn_block].reshape(received.shape[0], outer_count * attn_block)
    up_cols = received[:, :, attn_block : attn_block + unit_block].reshape(
        received.shape[0], outer_count * unit_block
    )
    act_cols = received[:, :, attn_block + unit_block :].reshape(
        received.shape[0], outer_count * unit_block
    )
    outer_ids = lax.iota(jnp.int32, outer_count)[:, None]
    inner_ids = lax.iota(jnp.int32, attn_block)[None, :]
    feature_ids = ((outer_ids * inner_count + inner_index) * attn_block + inner_ids).reshape(
        outer_count * attn_block
    )
    is_projection = (feature_ids < 3 * model_width)[None, :]
    start_sums = (
        jnp.zeros((outer_count * attn_block, model_width), jnp.float32),
        jnp.zeros((outer_count * unit_block, model_width), jnp.float32),
        jnp.zeros((outer_count * unit_block, model_width), jnp.float32),
    )
    piece_h1 = lax.all_gather(hidden_one, "rep", axis=0, tiled=True)
    piece_mixed = lax.all_gather(for_sending(mixed), "rep", axis=0, tiled=True)
    piece_h2 = lax.all_gather(hidden_two, "rep", axis=0, tiled=True)
    piece_dd = lax.all_gather(grad_down_in, "rep", axis=0, tiled=True)
    zero_low = jnp.zeros_like(attn_cols)
    left_proj = jnp.where(is_projection, attn_cols, zero_low)
    left_out = jnp.where(is_projection, zero_low, attn_cols)
    attn_total = (
        start_sums[0] + contract(left_proj, piece_h1, 0, 0) + contract(left_out, piece_mixed, 0, 0)
    )
    up_total = start_sums[1] + contract(up_cols, piece_h2, 0, 0)
    down_total = start_sums[2] + contract(act_cols, piece_dd, 0, 0)
    attn_shard, up_shard, down_shard = (
        lax.psum_scatter(attn_total, "fsdp", scatter_dimension=0, tiled=True),
        lax.psum_scatter(up_total, "fsdp", scatter_dimension=0, tiled=True),
        lax.psum_scatter(down_total, "fsdp", scatter_dimension=0, tiled=True),
    )
    grad_params = jnp.concatenate(
        [
            grad_gain_one,
            grad_shift_one,
            bias_sums[:model_width],
            bias_sums[2 * model_width :],
            grad_out_bias,
            grad_gain_two,
            grad_shift_two,
            grad_up_bias,
            grad_down_bias,
        ]
    )
    vector_shard = lax.psum_scatter(grad_params, ("fsdp", "rep"), scatter_dimension=0, tiled=True)
    return (
        output.astype(jnp.bfloat16),
        grad_inputs.astype(jnp.bfloat16),
        attn_shard,
        vector_shard,
        up_shard,
        down_shard,
    )


def solution(mesh):
    return jax.shard_map(
        local,
        mesh=mesh,
        in_specs=(
            P(("fsdp", "rep"), None),
            P(("fsdp", "rep"), None),
            P(("fsdp", "rep"), None),
            P(("fsdp", "rep")),
            P(("fsdp", "rep"), None),
            P(("fsdp", "rep"), None),
            P(("fsdp", "rep"), None),
        ),
        out_specs=(
            P(("fsdp", "rep"), None),
            P(("fsdp", "rep"), None),
            P(("fsdp", "rep"), None),
            P(("fsdp", "rep")),
            P(("fsdp", "rep"), None),
            P(("fsdp", "rep"), None),
        ),
        check_vma=False,
    )
```

```python
import jax
import jax.numpy as jnp
from jax import lax
from jax.experimental import pallas as pl
from jax.experimental.pallas import tpu as pltpu
from jax.sharding import PartitionSpec as P

HEADS = 17
HEAD_DIM = 64
FF = 4352
LANES = 128

epsilon = 1e-05
negative = -1e30
factor = HEAD_DIM ** (-0.5)
both = ("fsdp", "rep")


def contract(left, right, left_dim, right_dim):
    return lax.dot_general(
        left, right, (((left_dim,), (right_dim,)), ((), ())), preferred_element_type=jnp.float32
    )


def normalize(values):
    center = values - jnp.mean(values, axis=1, keepdims=True)
    scaled = lax.rsqrt(jnp.mean(center * center, axis=1, keepdims=True) + epsilon)
    return (center * scaled, scaled)


def norm_back(grad_normed, normed, scaled, gain):
    scaled_grad = grad_normed * gain
    return scaled * (
        scaled_grad
        - jnp.mean(scaled_grad, axis=1, keepdims=True)
        - normed * jnp.mean(scaled_grad * normed, axis=1, keepdims=True)
    )


def visible(key_segment, query_segment):
    shape = (key_segment.shape[0], query_segment.shape[1])
    key_ids = lax.broadcasted_iota(jnp.int32, shape, 0)
    query_ids = lax.broadcasted_iota(jnp.int32, shape, 1)
    return (key_segment == query_segment) & (key_ids <= query_ids)


def head_rows(part, head):
    return pl.ds((part * HEADS + head) * HEAD_DIM, HEAD_DIM)


def forward_kernel(qkv_ref, key_seg_ref, query_seg_ref, mixed_ref, total_ref):
    allowed = visible(key_seg_ref[...], query_seg_ref[...])
    for head in range(HEADS):
        queries = qkv_ref[head_rows(0, head), :]
        keys = qkv_ref[head_rows(1, head), :]
        values = qkv_ref[head_rows(2, head), :]
        scores = jnp.where(allowed, contract(keys.T, queries, 1, 0) * factor, negative)
        peak = jnp.max(scores, axis=0, keepdims=True)
        exp_scores = jnp.exp(scores - peak)
        total = jnp.sum(exp_scores, axis=0, keepdims=True)
        probs = (exp_scores / total).astype(jnp.bfloat16)
        mixed_ref[head_rows(0, head), :] = contract(values, probs, 1, 0).astype(jnp.bfloat16)
        total_ref[pl.ds(head, 1), :] = peak + jnp.log(total)


def backward_kernel(qkv_ref, total_ref, grad_ref, key_seg_ref, query_seg_ref, out_ref):
    allowed = visible(key_seg_ref[...], query_seg_ref[...])
    for head in range(HEADS):
        queries = qkv_ref[head_rows(0, head), :]
        keys = qkv_ref[head_rows(1, head), :]
        values = qkv_ref[head_rows(2, head), :]
        grads = grad_ref[head_rows(0, head), :]
        scores = contract(keys.T, queries, 1, 0) * factor
        probs = jnp.where(allowed, jnp.exp(scores - total_ref[pl.ds(head, 1), :]), 0.0)
        grad_probs = contract(values.T, grads, 1, 0)
        delta = jnp.sum(probs * grad_probs, axis=0, keepdims=True)
        grad_scores = (probs * (grad_probs - delta) * factor).astype(jnp.bfloat16)
        out_ref[head_rows(0, head), :] = contract(keys, grad_scores, 1, 0).astype(jnp.bfloat16)
        out_ref[head_rows(1, head), :] = contract(queries, grad_scores, 1, 1).astype(jnp.bfloat16)
        out_ref[head_rows(2, head), :] = contract(
            grads, probs.astype(jnp.bfloat16), 1, 1
        ).astype(jnp.bfloat16)


def on_chip(body, outs, args, flops):
    return pl.pallas_call(
        body,
        out_shape=outs,
        compiler_params=pltpu.CompilerParams(vmem_limit_bytes=32 * 2**20),
        cost_estimate=pl.CostEstimate(flops=flops, bytes_accessed=6 * 2**20, transcendentals=2**20),
    )(*args)


def local(tokens, lengths, attn_weights, vectors, up_weights, down_weights, cotangent):
    outer_count = lax.axis_size("fsdp")
    inner_count = lax.axis_size("rep")
    device_count = outer_count * inner_count
    slot_count, model_width = tokens.shape
    shard_rows = attn_weights.shape[0]
    vector_size = vectors.shape[0]
    vector_rows = -(-vector_size // (16 * model_width)) * 16
    vector_rows = vector_rows - (shard_rows % 16) if shard_rows % 16 else vector_rows
    packed_vectors = jnp.pad(vectors, (0, vector_rows * model_width - vector_size))
    packed = jnp.concatenate([attn_weights, packed_vectors.reshape(vector_rows, model_width)], axis=0)
    packed_full = lax.all_gather(packed, both, axis=0)
    up_full = lax.all_gather(up_weights, both, axis=0, tiled=True)
    down_full = lax.all_gather(down_weights, both, axis=0, tiled=True)
    attn_full = packed_full[:, :shard_rows].reshape(device_count * shard_rows, model_width)
    vector_full = packed_full[:, shard_rows:].reshape(device_count, vector_rows * model_width)
    params = vector_full[:, :vector_size].reshape(device_count * vector_size).astype(jnp.float32)
    qkv_full = attn_full[: 3 * model_width]
    out_full = attn_full[3 * model_width :]
    gain_one = params[0:model_width]
    shift_one = params[model_width : 2 * model_width]
    query_bias = params[2 * model_width : 3 * model_width]
    value_bias = params[3 * model_width : 4 * model_width]
    out_bias = params[4 * model_width : 5 * model_width]
    gain_two = params[5 * model_width : 6 * model_width]
    shift_two = params[6 * model_width : 7 * model_width]
    up_bias = params[7 * model_width : 7 * model_width + FF]
    down_bias = params[7 * model_width + FF :]

    seq_count = lengths.shape[1]
    upto = lax.iota(jnp.int32, seq_count)[:, None] >= lax.iota(jnp.int32, seq_count)[None, :]
    seq_ends = jnp.sum(jnp.where(upto, lengths, 0), axis=1)
    positions = lax.iota(jnp.int32, slot_count)
    segment = jnp.sum((positions[:, None] >= seq_ends[None, :]).astype(jnp.int32), axis=1)
    live_rows = (positions < seq_ends[-1]).astype(jnp.float32)[:, None]
    key_segment, query_segment = segment[:, None], segment[None, :]

    inputs = tokens.astype(jnp.float32)
    normed_one, scaled_one = normalize(inputs)
    hidden_one = (normed_one * gain_one + shift_one).astype(jnp.bfloat16)
    qkv_bias = jnp.concatenate([query_bias, jnp.zeros_like(query_bias), value_bias])
    qkv = (contract(qkv_full, hidden_one, 1, 1) + qkv_bias[:, None]).astype(jnp.bfloat16)
    mixed, totals = on_chip(
        forward_kernel,
        (
            jax.ShapeDtypeStruct((model_width, slot_count), jnp.bfloat16),
            jax.ShapeDtypeStruct((HEADS, slot_count), jnp.float32),
        ),
        (qkv, key_segment, query_segment),
        4 * slot_count * slot_count * model_width,
    )
    residual = inputs + contract(mixed, out_full, 0, 1) + out_bias
    normed_two, scaled_two = normalize(residual)
    hidden_two = (normed_two * gain_two + shift_two).astype(jnp.bfloat16)
    grad_output = cotangent.astype(jnp.float32) * live_rows
    grad_down_in = grad_output.astype(jnp.bfloat16)

    def to_all(right):
        copies = jnp.broadcast_to(right[None], (inner_count,) + right.shape)
        return lax.all_to_all(copies, "rep", split_axis=0, concat_axis=0, tiled=True)

    right_down = to_all(grad_down_in)
    right_one = to_all(hidden_one)
    right_mixed = to_all(mixed.T)
    up_full, right_down, right_one = lax.optimization_barrier((up_full, right_down, right_one))
    upward = contract(up_full, hidden_two, 1, 1) + up_bias[:, None]

    def gelu_exact(values):
        return jax.nn.gelu(values, approximate=False)

    activated, gelu_vjp = jax.vjp(gelu_exact, upward)
    activated = activated.astype(jnp.bfloat16)
    def to_owners(left):
        blocks = left.reshape(outer_count, inner_count, shard_rows, slot_count)
        blocks = blocks.transpose(1, 0, 2, 3).reshape(
            inner_count * outer_count * shard_rows, slot_count
        )
        return lax.all_to_all(blocks, "rep", split_axis=0, concat_axis=0, tiled=True).reshape(
            inner_count, outer_count * shard_rows, slot_count
        )

    def owner_grad(left, right):
        return sum(contract(left[i], right[i], 1, 0) for i in range(inner_count))

    def summed(partial):
        return lax.psum_scatter(
            partial.astype(jnp.bfloat16), "fsdp", scatter_dimension=0, tiled=True
        )

    act_rows = to_owners(activated)
    down_full, act_rows, right_mixed = lax.optimization_barrier((down_full, act_rows, right_mixed))
    right_two = to_all(hidden_two)
    down_shard = summed(owner_grad(act_rows, right_down))

    output = (residual + contract(activated, down_full, 0, 0) + down_bias) * live_rows
    grad_down_bias = jnp.sum(grad_down_in.astype(jnp.float32), axis=0)
    grad_act = contract(down_full, grad_down_in, 1, 1)
    grad_upward = gelu_vjp(grad_act)[0]
    grad_up_in = grad_upward.astype(jnp.bfloat16)
    grad_up_bias = jnp.sum(grad_up_in.astype(jnp.float32), axis=1)

    up_shard = summed(owner_grad(to_owners(grad_up_in), right_two))

    grad_hidden_two = contract(grad_up_in, up_full, 0, 0)
    grad_gain_two = jnp.sum(grad_hidden_two * normed_two, axis=0)
    grad_shift_two = jnp.sum(grad_hidden_two, axis=0)
    grad_residual = grad_output + norm_back(grad_hidden_two, normed_two, scaled_two, gain_two)
    grad_attended = grad_residual.astype(jnp.bfloat16)
    grad_out_bias = jnp.sum(grad_attended.astype(jnp.float32), axis=0)
    grad_mixed = contract(out_full, grad_attended, 0, 1).astype(jnp.bfloat16)
    grad_qkv = on_chip(
        backward_kernel,
        jax.ShapeDtypeStruct((3 * model_width, slot_count), jnp.bfloat16),
        (qkv, totals, grad_mixed, key_segment, query_segment),
        10 * slot_count * slot_count * model_width,
    )

    attn_left = to_owners(jnp.concatenate([grad_qkv, grad_attended.T], axis=0))
    feature_ids = (
        (lax.iota(jnp.int32, outer_count)[:, None] * inner_count + lax.axis_index("rep"))
        * shard_rows
        + lax.iota(jnp.int32, shard_rows)[None, :]
    ).reshape(1, outer_count * shard_rows, 1)
    is_projection = feature_ids < 3 * model_width
    zero_low = jnp.zeros_like(attn_left)
    attn_total = owner_grad(jnp.where(is_projection, attn_left, zero_low), right_one) + owner_grad(
        jnp.where(is_projection, zero_low, attn_left), right_mixed
    )
    attn_shard = summed(attn_total)

    bias_sums = jnp.sum(grad_qkv.astype(jnp.float32), axis=1)
    grad_hidden_one = contract(grad_qkv, qkv_full, 0, 0)
    grad_gain_one = jnp.sum(grad_hidden_one * normed_one, axis=0)
    grad_shift_one = jnp.sum(grad_hidden_one, axis=0)
    grad_inputs = grad_residual + norm_back(grad_hidden_one, normed_one, scaled_one, gain_one)

    grad_params = jnp.concatenate(
        [
            grad_gain_one,
            grad_shift_one,
            bias_sums[:model_width],
            bias_sums[2 * model_width :],
            grad_out_bias,
            grad_gain_two,
            grad_shift_two,
            grad_up_bias,
            grad_down_bias,
        ]
    )
    per_device = -(-vector_size // LANES) * LANES
    padded = jnp.pad(
        grad_params.reshape(device_count, vector_size), ((0, 0), (0, per_device - vector_size))
    )
    terms = lax.all_to_all(padded, both, split_axis=0, concat_axis=0, tiled=True)
    vector_shard = jnp.sum(terms, axis=0)[:vector_size]
    return (
        output.astype(jnp.bfloat16),
        grad_inputs.astype(jnp.bfloat16),
        attn_shard.astype(jnp.float32),
        vector_shard,
        up_shard.astype(jnp.float32),
        down_shard.astype(jnp.float32),
    )


def solution(mesh):
    rows = P(both, None)
    return jax.shard_map(
        local,
        mesh=mesh,
        in_specs=(rows, rows, rows, P(both), rows, rows, rows),
        out_specs=(rows, rows, rows, P(both), rows, rows),
        check_vma=False,
    )
```
